32 devices in a mesh: blocks: 8 (over z, x), cols: 4 (over y, core).
Axes of the slice: x: 2, y: 2, z: 4, core: 2. Of those that a mesh axis runs over, the one named last changes fastest.
Arguments:
- border: bfloat16 [512, 64, 2048], P('blocks', None, 'cols')
- block_inverse: bfloat16 [512, 64, 64], P('blocks'), as said below
- pattern: int32 [512, 32], P('blocks', 'cols'), may hold values 0 or 1
- rhs_blocks: float32 [512, 64], P('blocks'), may hold values from -6 to 6
- link_diag: float32 [2048], P('cols'), may hold values from 0.001 to 0.3
- link_rhs: float32 [2048], P('cols'), may hold values from -6 to 6
Outputs:
- block_step: float32 [512, 64], P('blocks')
- link_step: float32 [2048], P('cols')
The draws below stay inside these ranges and needn't reach their ends.
Inputs may be any that keep to these rules, and one draw needn't show every extreme that they name: `block_inverse`: each 64 x 64 block is symmetric and positive definite.
All inputs are finite; a program needn't handle non-finite values. No bound on the sum of `pattern` on one device may be relied on, other than what follows from the above.
Results may differ from the reference program's by a relative error of at most 0.0024.
Values may be sent and summed in bfloat16 or wider, within the bound.
A program may use at most 128 MiB of HBM per device.

```python
import math
import jax
import jax.numpy as jnp
from jax import lax

NB = 64
L = 2048
LB = 32
NBLK = 512


def draw_block_inverse(key, part):
    first_key, second_key = jax.random.split(jax.random.fold_in(key, 11))
    spread = 1.2 / NB
    diagonal = jnp.exp(jax.random.uniform(first_key, (NBLK, NB), jnp.float32, jnp.log(1.5), jnp.log(4.0)))
    raw = jax.random.uniform(second_key, (NBLK, NB, NB), jnp.float32, -1.0, 1.0)
    symmetric = 0.5 * (raw + jnp.swapaxes(raw, 1, 2)) * spread
    identity = jnp.eye(NB, dtype=jnp.float32)
    result = symmetric * (1.0 - identity) + diagonal[:, :, None] * identity
    return result.astype(jnp.bfloat16)


def draw_border(key, part):
    base_key = jax.random.fold_in(key, 23)
    order_key = jax.random.fold_in(base_key, 0)
    sign_key = jax.random.fold_in(base_key, 1)
    mixing_key = jax.random.fold_in(base_key, 2)
    noise_key = jax.random.fold_in(base_key, 3)
    scale_key = jax.random.fold_in(base_key, 5)
    overall = (NBLK * NB // 2) ** (-0.5)
    partner = jax.random.permutation(order_key, L)
    signs = jnp.where(jax.random.bernoulli(sign_key, 0.5, (L,)), 1.0, -1.0).astype(jnp.float32)
    mixing = signs * 0.88 * jax.random.uniform(mixing_key, (L,), jnp.float32)
    noise = jax.random.truncated_normal(noise_key, -4.0, 4.0, (NBLK, NB, L), jnp.float32)
    column_scale = jnp.exp(jax.random.uniform(scale_key, (L,), jnp.float32, jnp.log(0.5), jnp.log(2.0)))
    mixed = noise + mixing * noise[:, :, partner]
    return (mixed * (column_scale * overall)).astype(jnp.bfloat16)


def set_ends(array, own_key, smallest, high):
    extent = array.shape
    index_at = [jax.random.randint(jax.random.fold_in(own_key, axis), (), 0, extent[axis]) for axis in range(len(extent))]
    array = array.at[tuple(index_at)].set(smallest)
    longest = extent.index(max(extent))
    index_at[longest] = (index_at[longest] + 1) % extent[longest]
    return array.at[tuple(index_at)].set(high)


def levels(stream_key, shape, shards, least, largest):
    factor_of, own = 1.0, jax.random.fold_in(stream_key, 6)
    for dim, blocks in shards:
        draws = jnp.exp(jax.random.uniform(jax.random.fold_in(own, dim), (blocks,), jnp.float32, least / len(shards), largest / len(shards)))
        factor_of = factor_of * jnp.repeat(draws, shape[dim] // blocks).reshape([-1 if axis == dim else 1 for axis in range(len(shape))])
    return factor_of


def bell_draw(own_key, shape, scale, reach, pieces=(), kind=jnp.bfloat16):
    entries = scale * jax.random.normal(own_key, shape, jnp.float32)
    if pieces:
        entries = entries * levels(own_key, shape, pieces, -0.22, 0.18)
    return jnp.clip(entries, -reach, reach).astype(kind)


def setup_inputs(seed: int = 0) -> dict:
    streams_of = jax.random.split(jax.random.key(seed), 7)
    return {
        "border": draw_border(jax.random.fold_in(streams_of[6], 71), 0),
        "block_inverse": draw_block_inverse(jax.random.fold_in(streams_of[6], 71), 0),
        "pattern": set_ends((jax.random.randint(streams_of[2], (NBLK, LB), 0, 2) < 1).astype(jnp.int32), jax.random.fold_in(streams_of[2], 1), 0, 1),
        "rhs_blocks": bell_draw(streams_of[3], (NBLK, NB), 1.0, 6.0, ((0, 8),), jnp.float32),
        "link_diag": jnp.clip(jnp.exp(math.log(0.3) - 5.7037825 * jax.random.uniform(streams_of[4], (L,), jnp.float32) ** levels(streams_of[4], (L,), ((0, 4),), -0.2, 0.2)), 0.001, 0.3),
        "link_rhs": bell_draw(streams_of[5], (L,), 1.0, 6.0, ((0, 4),), jnp.float32),
    }


def apply_pattern(border, pattern):
    hours, order, width = border.shape
    panels = pattern.shape[1]
    shaped = border.reshape(hours, order, panels, width // panels)
    keep = pattern.astype(border.dtype)[:, None, :, None]
    return (shaped * keep).reshape(hours, order, width)

def reference(border, block_inverse, pattern, rhs_blocks, link_diag, link_rhs):
    masked = apply_pattern(border, pattern)
    total_rows = NBLK * NB
    inverse_wide = block_inverse.astype(jnp.float32)
    solved = jnp.einsum('bij,bjk->bik', inverse_wide, masked.astype(jnp.float32), precision=lax.Precision.HIGHEST).astype(jnp.bfloat16)
    weighted = jnp.einsum('bij,bj->bi', inverse_wide, rhs_blocks, precision=lax.Precision.HIGHEST)
    weighted_low = weighted.astype(jnp.bfloat16)
    flat_masked = masked.reshape(total_rows, L)
    product = jnp.dot(flat_masked.T.astype(jnp.float32), solved.reshape(total_rows, L).astype(jnp.float32), preferred_element_type=jnp.float32)
    complement = jnp.diag(link_diag) + 0.5 * (product + product.T)
    reduced_rhs = jnp.dot(weighted_low.reshape(1, total_rows).astype(jnp.float32), flat_masked.astype(jnp.float32), preferred_element_type=jnp.float32)[0] - link_rhs
    factor = jnp.linalg.cholesky(complement)
    link_step = jax.scipy.linalg.cho_solve((factor, True), reduced_rhs)
    link_low = link_step.astype(jnp.bfloat16)
    coupling = jnp.dot(flat_masked.astype(jnp.float32), link_low.astype(jnp.float32), preferred_element_type=jnp.float32).reshape(NBLK, NB)
    block_step = jnp.einsum('bij,bj->bi', inverse_wide, rhs_blocks - coupling, precision=lax.Precision.HIGHEST)
    return (block_step, link_step)
```

```python
import functools
import jax
import jax.numpy as jnp
from jax import lax
from jax.experimental import pallas as pl
from jax.experimental.pallas import tpu as pltpu
from jax.sharding import PartitionSpec as P

BLOCK = 128
STRIP = 256


def apply_pattern(border, pattern):
    hours, order, width = border.shape
    panels = pattern.shape[1]
    shaped = border.reshape(hours, order, panels, width // panels)
    keep = pattern.astype(border.dtype)[:, None, :, None]
    return (shaped * keep).reshape(hours, order, width)


def split_three(value):
    high = value.astype(jnp.bfloat16)
    rest = value - high.astype(jnp.float32)
    middle = rest.astype(jnp.bfloat16)
    low = (rest - middle.astype(jnp.float32)).astype(jnp.bfloat16)
    return high, middle, low


def invert_block(block_ref, order):
    groups = order // 8
    lane = lax.broadcasted_iota(jnp.int32, (8, order), 1)
    sub = lax.broadcasted_iota(jnp.int32, (8, order), 0)
    for group in range(groups):
        first = 8 * group
        inside = (lane >= first) & (lane < first + 8)
        own = block_ref[first : first + 8, :]
        corner = [jnp.broadcast_to(own[:, first + j : first + j + 1], (8, order)) for j in range(8)]
        own = jnp.where(inside, (lane == sub + first).astype(jnp.float32), own)
        for j in range(8):
            scale = 1.0 / corner[j][j : j + 1, :]
            factor = corner[j]
            row = own[j : j + 1, :] * scale
            own = jnp.where(sub == j, row, own - factor * row)
            for other in range(j + 1, 8):
                row = corner[other][j : j + 1, :] * scale
                corner[other] = jnp.where(sub == j, row, corner[other] - factor * row)
        for other in range(groups):
            if other == group:
                continue
            at = 8 * other
            theirs = block_ref[at : at + 8, :]
            total = jnp.where(inside, 0.0, theirs)
            for j in range(8):
                total = total - jnp.broadcast_to(theirs[:, first + j : first + j + 1], (8, order)) * own[j : j + 1, :]
            block_ref[at : at + 8, :] = total
        block_ref[first : first + 8, :] = own


def factor_kernel(extent, packed_ref, diag_ref, rhs_ref, out_ref, a_ref, left_ref, right_ref, rows_ref, wide_ref, block_ref, sems):
    nb, tile = BLOCK, STRIP
    strips = extent // tile
    steps = extent // nb
    per = tile // nb
    copies = []
    for strip in range(strips):
        fold = min(strip, strips - 1 - strip)
        start = 0 if strip == fold else (fold + 1) * tile
        width = (strip + 1) * tile
        copy = pltpu.make_async_copy(
            packed_ref.at[fold * tile : (fold + 1) * tile, start : start + width],
            a_ref.at[strip * tile : (strip + 1) * tile, 0:width],
            sems.at[strip],
        )
        copy.start()
        copies.append(copy)
    rows_ref[...] = jnp.broadcast_to(rhs_ref[...], rows_ref.shape)
    for copy in copies:
        copy.wait()
    eye = lax.broadcasted_iota(jnp.int32, (nb, nb), 0) == lax.broadcasted_iota(jnp.int32, (nb, nb), 1)
    nt = (((1,), (1,)), ((), ()))

    def forward(step, carry):
        base = pl.multiple_of(step * nb, nb)
        block_ref[...] = a_ref[pl.ds(base, nb), pl.ds(base, nb)] + jnp.where(eye, diag_ref[:, pl.ds(base, nb)], 0.0)
        invert_block(block_ref, nb)
        inverse = block_ref[...]
        a_ref[pl.ds(base, nb), pl.ds(base, nb)] = inverse
        first_tile = (step + 1) // per

        def panel(index, carry):
            at = pl.multiple_of(index * tile, tile)
            column = a_ref[pl.ds(at, tile), pl.ds(base, nb)]
            row_id = at + lax.broadcasted_iota(jnp.int32, (tile, nb), 0)
            column = jnp.where(row_id >= base + nb, column, 0.0)
            solved = jnp.dot(column, inverse, precision=lax.Precision.HIGHEST, preferred_element_type=jnp.float32)
            high, middle, low = split_three(column)
            left_ref[pl.ds(at, tile), :] = jnp.concatenate([high, high, middle, high, low, middle], axis=1)
            high, middle, low = split_three(solved)
            right_ref[pl.ds(at, tile), :] = jnp.concatenate([high, middle, high, low, high, middle], axis=1)
            return carry

        lax.fori_loop(first_tile, strips, panel, 0)
        high, middle, low = split_three(rows_ref[:, pl.ds(base, nb)])
        lead = jnp.concatenate([high, high, middle, high, low, middle], axis=1)

        def outer(index, carry):
            at = pl.multiple_of(index * tile, tile)
            theirs = right_ref[pl.ds(at, tile), :]
            rows_ref[:, pl.ds(at, tile)] -= lax.dot_general(lead, theirs, nt, preferred_element_type=jnp.float32)

            def inner(other, carry):
                to = pl.multiple_of(other * tile, tile)
                a_ref[pl.ds(to, tile), pl.ds(at, tile)] -= lax.dot_general(
                    left_ref[pl.ds(to, tile), :], theirs, nt, preferred_element_type=jnp.float32
                )
                return carry

            return lax.fori_loop(index, strips, inner, carry)

        return lax.fori_loop(first_tile, strips, outer, carry)

    lax.fori_loop(0, steps, forward, 0)

    def backward(count, carry):
        step = steps - 1 - count
        base = pl.multiple_of(step * nb, nb)

        def gather(index, total):
            at = pl.multiple_of(index * nb, nb)
            part = a_ref[pl.ds(at, nb), pl.ds(base, nb)] * wide_ref[pl.ds(at, nb), :]
            return total + jnp.sum(part.reshape(nb // 8, 8, nb), axis=0)

        total = lax.fori_loop(step + 1, steps, gather, jnp.zeros((8, nb), jnp.float32))
        target = rows_ref[0:1, pl.ds(base, nb)] - jnp.sum(total, axis=0, keepdims=True)
        tall = jnp.transpose(jnp.broadcast_to(target, (nb, nb)))
        piece = jnp.sum(a_ref[pl.ds(base, nb), pl.ds(base, nb)] * tall, axis=0, keepdims=True)
        out_ref[:, pl.ds(base, nb)] = piece
        wide_ref[pl.ds(base, nb), :] = jnp.transpose(jnp.broadcast_to(piece, (nb, nb)))
        return carry

    lax.fori_loop(0, steps, backward, 0)


def solve_packed(packed, diag, rhs):
    extent = diag.shape[0]
    out = pl.pallas_call(
        functools.partial(factor_kernel, extent),
        out_shape=jax.ShapeDtypeStruct((1, extent), jnp.float32),
        in_specs=[
            pl.BlockSpec(memory_space=pl.ANY),
            pl.BlockSpec(memory_space=pltpu.VMEM),
            pl.BlockSpec(memory_space=pltpu.VMEM),
        ],
        out_specs=pl.BlockSpec(memory_space=pltpu.VMEM),
        scratch_shapes=[
            pltpu.VMEM((extent, extent), jnp.float32),
            pltpu.VMEM((extent, 6 * BLOCK), jnp.bfloat16),
            pltpu.VMEM((extent, 6 * BLOCK), jnp.bfloat16),
            pltpu.VMEM((16, extent), jnp.float32),
            pltpu.VMEM((extent, BLOCK), jnp.float32),
            pltpu.VMEM((BLOCK, BLOCK), jnp.float32),
            pltpu.SemaphoreType.DMA((extent // STRIP,)),
        ],
        compiler_params=pltpu.CompilerParams(vmem_limit_bytes=40 * 1024 * 1024),
    )(packed, diag.reshape(1, extent), rhs.reshape(1, extent))
    return out[0]


def per_device(border, block_inverse, pattern, rhs_blocks, link_diag, link_rhs):
    masked = apply_pattern(border, pattern)
    hours, order, own_width = masked.shape
    groups = lax.axis_size("cols")
    width = own_width * groups
    column = lax.axis_index("cols")
    offset = column * own_width
    inverse_wide = block_inverse.astype(jnp.float32)
    weighted = jnp.einsum("bij,bj->bi", inverse_wide, rhs_blocks, precision=lax.Precision.HIGHEST)
    weighted_low = weighted.astype(jnp.bfloat16)
    flat_masked = masked.reshape(hours * order, own_width)
    partial_rhs = jnp.dot(
        weighted_low.reshape(1, hours * order), flat_masked, preferred_element_type=jnp.float32
    )[0]
    contract = (((0,), (0,)), ((), ()))
    quarter = hours // groups
    mine = lax.all_to_all(masked, "cols", split_axis=0, concat_axis=2, tiled=True)
    inverse_mine = lax.dynamic_slice_in_dim(block_inverse, column * quarter, quarter, 0)
    solved_mine = jnp.einsum(
        "bij,bjk->bik", inverse_mine, mine, preferred_element_type=jnp.float32
    ).astype(jnp.bfloat16)
    flat_mine = mine.reshape(quarter * order, width)
    flat_solved = solved_mine.reshape(quarter * order, width)
    strips = width // STRIP
    left = jnp.concatenate([flat_mine, flat_solved], axis=0)
    right = jnp.concatenate([flat_solved, flat_mine], axis=0)
    bands = [
        0.5
        * lax.dot_general(
            left[:, s * STRIP : (s + 1) * STRIP],
            right[:, : (s + 1) * STRIP],
            contract,
            preferred_element_type=jnp.float32,
        )
        for s in range(strips)
    ]
    folded = jnp.concatenate(
        [jnp.concatenate([bands[s], bands[strips - 1 - s]], axis=1) for s in range(strips // 2)], axis=0
    )
    share = lax.psum_scatter(folded, "cols", scatter_dimension=0, tiled=True)
    part_sum = lax.psum_scatter(share, "blocks", scatter_dimension=0, tiled=True)
    packed = lax.all_gather(part_sum, ("cols", "blocks"), axis=0, tiled=True)
    own_rhs = lax.psum(partial_rhs, "blocks") - link_rhs
    vectors = lax.all_gather(jnp.stack([own_rhs, link_diag])[None], "cols", axis=0, tiled=True)
    vectors = jnp.transpose(vectors, (1, 0, 2)).reshape(2, width)
    link_full = solve_packed(packed, vectors[1], vectors[0])
    link_low = link_full.astype(jnp.bfloat16)
    own_low = lax.dynamic_slice_in_dim(link_low, offset, own_width, 0)
    partial_coupling = jnp.dot(flat_masked, own_low, preferred_element_type=jnp.float32).reshape(
        hours, order
    )
    coupling = lax.psum(partial_coupling, "cols")
    block_step = jnp.einsum(
        "bij,bj->bi", inverse_wide, rhs_blocks - coupling, precision=lax.Precision.HIGHEST
    )
    return (block_step, lax.dynamic_slice_in_dim(link_full, offset, own_width, 0))


def solution(mesh):
    placed = (
        P("blocks", None, "cols"),
        P("blocks", None, None),
        P("blocks", "cols"),
        P("blocks", None),
        P("cols"),
        P("cols"),
    )
    return jax.shard_map(
        per_device,
        mesh=mesh,
        in_specs=placed,
        out_specs=(P("blocks", None), P("cols")),
        check_vma=False,
    )
```
